32 devices in a mesh: section: 4 (over x, core), dp: 8 (over z, y).
Axes of the slice: x: 2, y: 2, z: 4, core: 2. Of those that a mesh axis runs over, the one named last changes fastest.
Arguments:
- inputs: bfloat16 [16, 896, 768], P('dp'), may hold values from -6 to 6
- blocks: bfloat16 [4, 6, 768, 768], P('section'), may hold values from -8 to 8
- norm_gain: float32 [4, 768], P('section'), may hold values from 0.1 to 1.9
- norm_bias: float32 [4, 768], P('section'), may hold values from -2 to 2
- segments: int32 [16, 896], P('dp'), may hold values from 0 to 3, never falling along the last dimension, each value on 1 to 448 neighbouring positions
- cotangent: bfloat16 [16, 896, 768], P('dp'), may hold values from -6 to 6
Outputs:
- section_outputs: bfloat16 [4, 16, 896, 768], P('section', 'dp')
- section_input_grads: bfloat16 [4, 16, 896, 768], P('section', 'dp')
- grad_blocks: float32 [4, 6, 768, 768], P('section', None, 'dp')
- grad_gain: float32 [4, 768], P('section', 'dp')
- grad_bias: float32 [4, 768], P('section', 'dp')
The draws below stay inside these ranges and needn't reach their ends.
Inputs may be any that keep to these rules, and one draw needn't show every extreme that they name: `segments`: along each row the gene number never falls; each gene spans 1 to 448 codons, and in each row one spans exactly that many.
All inputs are finite; a program needn't handle non-finite values.
Results may differ from the reference program's by a relative error of at most 0.015.
Values may be sent and summed in bfloat16 or wider, within the bound.
A program may use at most 192 MiB of HBM per device.

```python
import math
import jax
import jax.numpy as jnp
import numpy as np
from jax import lax

D = 768
HEADS = 12
HEAD_DIM = 64
FF = 3072
ROW = 896
ROWS = 16
N_SECTION = 4


def draw_blocks(key, part):
    key = jax.random.fold_in(key, 11)
    drawn = jnp.clip(jax.random.normal(key, (N_SECTION, 6, D, D), jnp.float32), -6.0, 6.0)
    down_scale = (D / FF) ** 0.5
    attention_scales = jnp.array([1.0, 1.0, 1.0, 8.0, 1.0, down_scale], jnp.float32)
    feed_scales = jnp.array([1.0, 1.0, 1.0, down_scale, down_scale, down_scale], jnp.float32)
    parity = (jnp.arange(N_SECTION) % 2)[:, None]
    scales = jnp.where(parity == 0, attention_scales[None, :], feed_scales[None, :]) * D ** (-0.5)
    return (drawn * scales[:, :, None, None]).astype(jnp.bfloat16)


def steps_of(key, extent, cuts, low, high):
    factor_of, own = 1.0, jax.random.fold_in(key, 6)
    for position, parts in cuts:
        heights = jnp.exp(jax.random.uniform(jax.random.fold_in(own, position), (parts,), jnp.float32, low / len(cuts), high / len(cuts)))
        factor_of = factor_of * jnp.repeat(heights, extent[position] // parts).reshape([-1 if axis == position else 1 for axis in range(len(extent))])
    return factor_of


def length_profile(number_of, total, limit, skew):
    weights = [(1 << 20) // math.isqrt(standing ** skew) + 1 for standing in range(2, number_of + 1)]
    surplus, given = total - limit - (number_of - 1), [1] * (number_of - 1)
    while surplus > 0:
        movable = [i for i in range(number_of - 1) if given[i] < limit]
        pool, remaining = sum([weights[i] for i in movable]), surplus
        for i in movable:
            more = min(limit - given[i], max(1, remaining * weights[i] // pool), surplus)
            given[i] = given[i] + more
            surplus = surplus - more
    return np.array([limit] + given)


def ragged(stream_key, amount, total, most, lean):
    if amount == 2:
        one = jax.random.randint(stream_key, (), max(1, total - most), min(most, total - 1) + 1)
        return jnp.stack([one, total - one])
    lengths = jnp.asarray(length_profile(amount, total, most, lean), jnp.int32)
    pairs = (amount - 1) // 2
    donor, sink = lengths[1:1 + 2 * pairs:2], lengths[2:2 + 2 * pairs:2]
    margin = jnp.minimum(donor - 1, most - sink)
    moved = jax.random.randint(jax.random.fold_in(stream_key, 1), (pairs,), 0, 1 << 20) % (margin + 1)
    lengths = lengths.at[1:1 + 2 * pairs:2].set(donor - moved).at[2:2 + 2 * pairs:2].set(sink + moved)
    return lengths[jax.random.permutation(jax.random.fold_in(stream_key, 2), amount)]


def scatter_about(own_key, dims, scale, most, split=(), held_as=jnp.bfloat16):
    values = scale * jax.random.normal(own_key, dims, jnp.float32)
    if split:
        values = values * steps_of(own_key, dims, split, -0.22, 0.18)
    return jnp.clip(values, -most, most).astype(held_as)


def setup_inputs(seed: int = 0) -> dict:
    key_list = jax.random.split(jax.random.key(seed), 7)
    return {
        "inputs": scatter_about(key_list[0], (ROWS, ROW, D), 1.0, 6.0, ((0, 8),)),
        "blocks": draw_blocks(jax.random.fold_in(key_list[6], 71), 0),
        "norm_gain": jnp.clip(1.0 + 0.18 * jax.random.normal(key_list[2], (N_SECTION, D), jnp.float32), 0.1, 1.9),
        "norm_bias": scatter_about(key_list[3], (N_SECTION, D), 0.3, 2.0, ((0, 4),), jnp.float32),
        "segments": jax.vmap(lambda own: jnp.searchsorted(jnp.cumsum(ragged(own, 4, ROW, ROW // 2, 0)), jnp.arange(ROW), side="right"))(jax.random.split(key_list[4], ROWS)).reshape((ROWS, ROW)).astype(jnp.int32),
        "cotangent": scatter_about(key_list[5], (ROWS, ROW, D), 1.0, 6.0, ((0, 8),)),
    }


@jax.custom_vjp
def low(v):
    return lax.optimization_barrier(v.astype(jnp.bfloat16)).astype(jnp.float32)

@jax.custom_vjp
def low_back(v):
    return v

def low_keep(v):
    return (low(v), None)

def low_pass(kept, grad):
    return (grad,)

def back_keep(v):
    return (v, None)

def back_low(kept, grad):
    return (low(grad),)
low.defvjp(low_keep, low_pass)
low_back.defvjp(back_keep, back_low)
norm_epsilon = 1e-05
masked_score = -1e+30
highest_precision = lax.Precision.HIGHEST

def layer_norm(values, gain_row, shift_row):
    average = lax.optimization_barrier(jnp.mean(values, axis=-1, keepdims=True))
    centred = values - average
    spread = lax.optimization_barrier(jnp.mean(centred * centred, axis=-1, keepdims=True))
    return centred * lax.rsqrt(spread + norm_epsilon) * gain_row + shift_row

def rotary_tables(segment_row):
    length = segment_row.shape[0]
    places = jnp.arange(length, dtype=jnp.int32)
    boundary = jnp.concatenate([jnp.ones((1,), dtype=jnp.bool_), segment_row[1:] != segment_row[:-1]])
    starts = lax.cummax(jnp.where(boundary, places, 0), axis=0)
    offsets = (places - starts).astype(jnp.float32)
    halves = jnp.arange(HEAD_DIM // 2, dtype=jnp.float32)
    frequency = jnp.power(10000.0, -2.0 * halves / HEAD_DIM)
    angles = offsets[:, None] * frequency[None, :]
    angles = jnp.concatenate([angles, angles], axis=-1)
    return (jnp.cos(angles), jnp.sin(angles))

def turn_rows(values, cosines, sine_rows):
    halfway = HEAD_DIM // 2
    turned = jnp.concatenate([-values[..., halfway:], values[..., :halfway]], axis=-1)
    return values * cosines[:, :, None, :] + turned * sine_rows[:, :, None, :]

def attend_row(packed):
    query_rows, key_rows, value_rows, segment_row = packed
    raw_scores = jnp.einsum('qhd,khd->hqk', query_rows, key_rows, precision=highest_precision)
    scores = low_back(raw_scores) * HEAD_DIM ** (-0.5)
    same_gene = segment_row[:, None] == segment_row[None, :]
    scores = jnp.where(same_gene[None], scores, masked_score)
    highest = lax.optimization_barrier(jnp.max(scores, axis=-1, keepdims=True))
    raised = jnp.exp(scores - highest)
    weights = low(raised / lax.optimization_barrier(jnp.sum(raised, axis=-1, keepdims=True)))
    return jnp.einsum('hqk,khd->qhd', weights, value_rows, precision=highest_precision)

def attention_section(hidden, w_qkv, w_out, gain_row, shift_row, segments):
    row_count, length, width = hidden.shape
    normed = low(layer_norm(hidden, gain_row, shift_row))
    projected = jnp.einsum('nli,ij->nlj', normed, w_qkv, precision=highest_precision)
    cosines, sine_rows = jax.vmap(rotary_tables)(segments)
    head_shape = (row_count, length, HEADS, HEAD_DIM)
    query_rows = low(turn_rows(low_back(projected[..., :width]).reshape(head_shape), cosines, sine_rows))
    key_rows = low(turn_rows(low_back(projected[..., width:2 * width]).reshape(head_shape), cosines, sine_rows))
    value_rows = low(low_back(projected[..., 2 * width:])).reshape(head_shape)
    mixture = lax.map(jax.checkpoint(attend_row), (query_rows, key_rows, value_rows, segments))
    mixture = low(low_back(mixture.reshape(row_count, length, width)))
    return hidden + jnp.einsum('nli,ij->nlj', mixture, w_out, precision=highest_precision)

def feed_section(hidden, w_up, w_down, gain_row, shift_row):
    normed = low(layer_norm(hidden, gain_row, shift_row))
    before = low_back(jnp.einsum('nli,ij->nlj', normed, w_up, precision=highest_precision))
    activated = low(jax.nn.gelu(before, approximate=False))
    return hidden + jnp.einsum('nlj,ji->nli', activated, w_down, precision=highest_precision)

def reference(inputs, blocks, norm_gain, norm_bias, segments, cotangent):
    source = inputs.astype(jnp.float32)
    weights = blocks.astype(jnp.float32)
    nudges = jnp.zeros((N_SECTION,) + inputs.shape, jnp.float32)

    def forward(source, weights, gain_rows, shift_rows, nudges):
        hidden = source
        results = []
        for section_index in range(N_SECTION):
            entering = low_back(hidden + nudges[section_index])
            own_blocks = weights[section_index]
            if section_index % 2 == 0:
                w_qkv = jnp.concatenate([own_blocks[0], own_blocks[1], own_blocks[2]], axis=1)
                leaving = attention_section(entering, w_qkv, own_blocks[3], gain_rows[section_index], shift_rows[section_index], segments)
            else:
                lender = weights[section_index - 1]
                w_up = jnp.concatenate([lender[4], own_blocks[0], own_blocks[1], own_blocks[2]], axis=1)
                w_down = jnp.concatenate([lender[5], own_blocks[3], own_blocks[4], own_blocks[5]], axis=0)
                leaving = feed_section(entering, w_up, w_down, gain_rows[section_index], shift_rows[section_index])
            hidden = low(leaving)
            results.append(hidden)
        return tuple(results)
    outputs, pullback = jax.vjp(forward, source, weights, norm_gain.astype(jnp.float32), norm_bias.astype(jnp.float32), nudges)
    cotangents = tuple((jnp.zeros_like(produced) for produced in outputs[:-1])) + (cotangent.astype(jnp.float32),)
    gradients = pullback(cotangents)
    return (jnp.stack(outputs).astype(jnp.bfloat16), gradients[4].astype(jnp.bfloat16), gradients[1], gradients[2], gradients[3])
```

```python
import functools
import jax
import jax.numpy as jnp
from jax import lax
from jax.experimental import pallas as pl
from jax.experimental.pallas import tpu as pltpu
from jax.sharding import PartitionSpec as P

HEAD_DIM = 64
EPSILON = 1e-05
MASKED = -1e30
F32 = jnp.float32
BF16 = jnp.bfloat16
CHUNK = 512


def dot_nn(a, b):
    return lax.dot_general(a, b, (((1,), (0,)), ((), ())), preferred_element_type=F32)


def dot_nt(a, b):
    return lax.dot_general(a, b, (((1,), (1,)), ((), ())), preferred_element_type=F32)


def dot_tn(a, b):
    return lax.dot_general(a, b, (((0,), (0,)), ((), ())), preferred_element_type=F32)


def normed_rows(x):
    mean = jnp.mean(x, axis=-1, keepdims=True)
    centred = x - mean
    scale = lax.rsqrt(jnp.mean(centred * centred, axis=-1, keepdims=True) + EPSILON)
    return centred * scale, scale


def norm_forward(x, gain, shift):
    xhat, _ = normed_rows(x)
    return (xhat * gain + shift).astype(BF16)


def norm_backward(x, dn, gain):
    xhat, scale = normed_rows(x)
    e = dn * gain
    mean_e = jnp.mean(e, axis=-1, keepdims=True)
    mean_ex = jnp.mean(e * xhat, axis=-1, keepdims=True)
    dx = (e - mean_e - xhat * mean_ex) * scale
    return dx, jnp.sum(dn * xhat, axis=0, keepdims=True), jnp.sum(dn, axis=0, keepdims=True)


def gelu_pair(x):
    half_square = (x * x) * (-0.5 * 1.4426950408889634)
    e = jnp.exp2(half_square)
    t = 1.0 / (1.0 + (0.3275911 * 0.7071067811865476) * jnp.abs(x))
    poly = ((((1.061405429 * t - 1.453152027) * t + 1.421413741) * t - 0.284496736) * t + 0.254829592) * t
    tail = 0.5 * poly * e
    cdf = jnp.where(x < 0, tail, 1.0 - tail)
    return x * cdf, cdf + x * e * 0.3989422804014327


def turned(u):
    lane = lax.broadcasted_iota(jnp.int32, u.shape, 1)
    first = lax.rem(lane, HEAD_DIM) < HEAD_DIM // 2
    return jnp.where(first, pltpu.roll(u, 128 - 32, 1), pltpu.roll(u, 32, 1))


def feed_forward(u, x_ref, n_ref, pool, w1, w2, gain, shift, put):
    x = x_ref[u].astype(F32)
    n_ref[u] = norm_forward(x, gain[...], shift[...])

    @pl.loop(0, 6)
    def _(j):
        cols = pl.ds(pl.multiple_of(j * CHUNK, CHUNK), CHUNK)
        a0 = dot_nn(n_ref[u], w1[:, cols])
        a, slope = gelu_pair(a0)
        pool[j * 4 + u] = slope.astype(BF16)
        pool[24 + j * 4 + u] = a.astype(BF16)

    for c in range(3):
        cols = slice(c * 256, c * 256 + 256)
        a = jnp.concatenate([pool[24 + j * 4 + u] for j in range(6)], axis=1)
        put(c, cols, (x_ref[u, :, cols].astype(F32) + dot_nn(a, w2[:, cols])).astype(BF16))


def feed_backward(u, x_ref, g_ref, pool, w1, w2, gain, norms, dn_ref, put):
    @pl.loop(0, 6)
    def _(j):
        rows = pl.ds(pl.multiple_of(j * CHUNK, CHUNK), CHUNK)
        da = dot_nt(g_ref[u], w2[rows, :])
        slot = j * 4 + u
        pool[slot] = (da * pool[slot].astype(F32)).astype(BF16)

    for c in range(3):
        rows = slice(c * 256, c * 256 + 256)
        da0 = jnp.concatenate([pool[j * 4 + u] for j in range(6)], axis=1)
        dn_ref[:, rows] = dot_nt(da0, w1[rows, :])
    finish_backward(u, x_ref, g_ref, gain, norms, dn_ref, put)


def finish_backward(u, x_ref, g_ref, gain, norms, dn_ref, put):
    dx, grad_gain, grad_shift = norm_backward(x_ref[u].astype(F32), dn_ref[...], gain[...])
    norms[0:1, :] += grad_gain
    norms[1:2, :] += grad_shift
    put((g_ref[u].astype(F32) + dx).astype(BF16))


def attention_forward(u, x_ref, n_ref, q_ref, k_ref, v_ref, o_ref, pool, w1, cos_ref, sin_ref, bias_ref, gain, shift, put):
    x = x_ref[u].astype(F32)
    n_ref[u] = norm_forward(x, gain[...], shift[...])
    for part, dest in ((0, q_ref), (1, k_ref)):
        for t in range(3):
            u2 = dot_nn(n_ref[u], w1[:, part * 768 + t * 256: part * 768 + t * 256 + 256])
            for s in range(2):
                w = u2[:, s * 128: s * 128 + 128]
                dest[u, :, t * 256 + s * 128: t * 256 + s * 128 + 128] = (w * cos_ref[u] + turned(w) * sin_ref[u]).astype(BF16)
    v_ref[u] = dot_nn(n_ref[u], w1[:, 1536:2304]).astype(BF16)

    @pl.loop(0, 6)
    def _(p):
        cols = pl.ds(pl.multiple_of(p * 128, 128), 128)
        q, k, v = q_ref[u, :, cols], k_ref[u, :, cols], v_ref[u, :, cols]
        low = lax.broadcasted_iota(jnp.int32, q.shape, 1) < HEAD_DIM
        outs = []
        for h in range(2):
            mine = low if h == 0 else jnp.logical_not(low)
            scores = dot_nt(jnp.where(mine, q, jnp.zeros_like(q)) * BF16(0.125), k) + bias_ref[...]
            raised = jnp.exp(scores - jnp.max(scores, axis=-1, keepdims=True))
            weights = (raised * (1.0 / jnp.sum(raised, axis=-1, keepdims=True))).astype(BF16)
            pool[u * 12 + p * 2 + h, :, 0:448] = weights
            outs.append(dot_nn(weights, v))
        o_ref[u, :, cols] = jnp.where(low, outs[0], outs[1]).astype(BF16)

    for c in range(3):
        cols = slice(c * 256, c * 256 + 256)
        put(c, cols, (x_ref[u, :, cols].astype(F32) + dot_nn(o_ref[u], w1[:, 2304 + c * 256: 2560 + c * 256])).astype(BF16))


def attention_backward(u, x_ref, g_ref, q_ref, k_ref, v_ref, o_ref, pool, w1, cos_ref, sin_ref, do_ref, gain, norms, dn_ref, put):
    do_ref[...] = dot_nt(g_ref[u], w1[:, 2304:3072]).astype(BF16)

    @pl.loop(0, 6)
    def _(p):
        cols = pl.ds(pl.multiple_of(p * 128, 128), 128)
        q, k, v, o = q_ref[u, :, cols], k_ref[u, :, cols], v_ref[u, :, cols], o_ref[u, :, cols]
        do = do_ref[:, cols]
        low = lax.broadcasted_iota(jnp.int32, q.shape, 1) < HEAD_DIM
        dqs, dks, dvs = [], [], []
        for h in range(2):
            mine = low if h == 0 else jnp.logical_not(low)
            do8 = jnp.where(mine, do, jnp.zeros_like(do)) * BF16(0.125)
            delta = jnp.sum(do8.astype(F32) * o.astype(F32), axis=-1, keepdims=True)
            weights = pool[u * 12 + p * 2 + h, :, 0:448]
            ds = (weights.astype(F32) * (dot_nt(do8, v) - delta)).astype(BF16)
            dqs.append(dot_nn(ds, k))
            dks.append(dot_tn(ds, q))
            dvs.append(dot_tn(weights, do))
        cos, sin = cos_ref[u], sin_ref[u]
        dq = jnp.where(low, dqs[0], dqs[1])
        dk = jnp.where(low, dks[0], dks[1])
        q_ref[u, :, cols] = (dq * cos - turned(dq) * sin).astype(BF16)
        k_ref[u, :, cols] = (dk * cos - turned(dk) * sin).astype(BF16)
        v_ref[u, :, cols] = jnp.where(low, dvs[0], dvs[1]).astype(BF16)

    for c in range(3):
        rows = slice(c * 256, c * 256 + 256)
        dqkv = jnp.concatenate([q_ref[u], k_ref[u], v_ref[u]], axis=1)
        dn_ref[:, rows] = dot_nt(dqkv, w1[rows, 0:2304])
    finish_backward(u, x_ref, g_ref, gain, norms, dn_ref, put)


MESH = pl.DeviceIdType.MESH
UNIT = 448
UNITS = 4


def relay_kernel(
    sections, x_hbm, cot_hbm, blocks_hbm, gain_hbm, shift_hbm, cos_hbm, sin_hbm, segc_hbm, segr_hbm,
    y_hbm, dx_hbm, grads_hbm, norms_hbm,
    x_ref, n_ref, g_ref, q_ref, k_ref, v_ref, o_ref, pool, w1, w2, cos_ref, sin_ref, segc, segr, bias, do_ref, dn_ref,
    gain, shift, norms,
    fsend, frecv, bsend, brecv, lsend, lrecv, load, wload, yout, dxout, gout,
):
    me = lax.axis_index("section")
    line = lax.axis_index("dp")
    ahead, behind = lax.rem(me + 1, sections), lax.rem(me + sections - 1, sections)
    first, last = me == 0, me == sections - 1
    attention = lax.rem(me, 2) == 0
    feed = jnp.logical_not(attention)

    barrier = pltpu.get_barrier_semaphore()
    for other in (ahead, behind):
        pl.semaphore_signal(barrier, inc=1, device_id=(other, line), device_id_type=MESH)

    small = [
        pltpu.make_async_copy(src, dst, load.at[i])
        for i, (src, dst) in enumerate(((gain_hbm, gain), (shift_hbm, shift)))
    ]
    tables = [
        pltpu.make_async_copy(src, dst, load.at[2 + i])
        for i, (src, dst) in enumerate(((cos_hbm, cos_ref), (sin_hbm, sin_ref), (segc_hbm, segc), (segr_hbm, segr)))
    ]

    def x_load(u):
        return pltpu.make_async_copy(x_hbm.at[u], x_ref.at[u], frecv.at[u])

    def g_load(u):
        return pltpu.make_async_copy(cot_hbm.at[u], g_ref.at[u], brecv.at[u])

    def attention_weight(i):
        return pltpu.make_async_copy(blocks_hbm.at[i], w1.at[:, i * 768:(i + 1) * 768], wload.at[i])

    def feed_weight(i):
        dst = w1.at[:, (i + 1) * 768:(i + 2) * 768] if i < 3 else w2.at[(i - 2) * 768:(i - 1) * 768, :]
        return pltpu.make_async_copy(blocks_hbm.at[i], dst, wload.at[i])

    def lent_weight(i):
        dst = w1.at[:, 0:768] if i == 0 else w2.at[0:768, :]
        return pltpu.make_async_remote_copy(
            src_ref=blocks_hbm.at[4 + i], dst_ref=dst, send_sem=lsend.at[i], recv_sem=lrecv.at[i],
            device_id=(ahead, line), device_id_type=MESH)

    def forward_send(u, src):
        return pltpu.make_async_remote_copy(
            src_ref=src, dst_ref=x_ref.at[u], send_sem=fsend.at[u], recv_sem=frecv.at[u],
            device_id=(ahead, line), device_id_type=MESH)

    def backward_send(u):
        return pltpu.make_async_remote_copy(
            src_ref=x_ref.at[u], dst_ref=g_ref.at[u], send_sem=bsend.at[u], recv_sem=brecv.at[u],
            device_id=(behind, line), device_id_type=MESH)

    def y_store(u, src):
        return pltpu.make_async_copy(src, y_hbm.at[u], yout.at[u])

    def dx_store(u):
        return pltpu.make_async_copy(x_ref.at[u], dx_hbm.at[u], dxout.at[u])

    @pl.when(first)
    def _():
        x_load(0).start()

    for copy in small:
        copy.start()

    @pl.when(attention)
    def _():
        for i in range(4):
            attention_weight(i).start()
        for copy in tables:
            copy.start()

    @pl.when(feed)
    def _():
        for i in range(6):
            feed_weight(i).start()

    @pl.when(first)
    def _():
        for u in range(1, UNITS):
            x_load(u).start()

    @pl.when(last)
    def _():
        for u in range(UNITS):
            g_load(u).start()

    pl.semaphore_wait(barrier, 2)

    @pl.when(attention)
    def _():
        for i in range(2):
            lent_weight(i).start()

    norms[...] = jnp.zeros(norms.shape, F32)
    for copy in small:
        copy.wait()

    @pl.when(attention)
    def _():
        for copy in tables:
            copy.wait()
        for i in range(4):
            attention_weight(i).wait()

    @pl.when(feed)
    def _():
        for i in range(6):
            feed_weight(i).wait()
        for i in range(2):
            lent_weight(i).wait_recv()

    def y_slot(u):
        return w2.at[pl.ds(pl.multiple_of(u * UNIT, UNIT), UNIT), :]

    def await_x(u):
        @pl.when(first)
        def _():
            x_load(u).wait()

        @pl.when(jnp.logical_not(first))
        def _():
            forward_send(u, x_ref.at[u]).wait_recv()

    def await_g(u):
        @pl.when(last)
        def _():
            g_load(u).wait()

        @pl.when(jnp.logical_not(last))
        def _():
            backward_send(u).wait_recv()

    def pass_y(u, src):
        @pl.when(jnp.logical_not(last))
        def _():
            forward_send(u, src).start()
        y_store(u, src).start()

    def pass_dx(u):
        @pl.when(jnp.logical_not(first))
        def _():
            backward_send(u).start()
        dx_store(u).start()

    def put_dx(u):
        def put(value):
            x_ref[u] = value
        return put

    def attention_f(u):
        await_x(u)
        bias[...] = jnp.where(segc[u] == segr[u], 0.0, MASKED)

        def put(c, cols, value):
            w2[pl.ds(pl.multiple_of(u * UNIT, UNIT), UNIT), cols] = value
        attention_forward(u, x_ref, n_ref, q_ref, k_ref, v_ref, o_ref, pool, w1, cos_ref, sin_ref, bias, gain, shift, put)
        pass_y(u, y_slot(u))

    def attention_b(u):
        await_g(u)
        attention_backward(u, x_ref, g_ref, q_ref, k_ref, v_ref, o_ref, pool, w1, cos_ref, sin_ref, do_ref, gain, norms, dn_ref, put_dx(u))
        pass_dx(u)

    def feed_f(u):
        await_x(u)

        def put(c, cols, value):
            q_ref[u, :, cols] = value
        feed_forward(u, x_ref, n_ref, pool, w1, w2, gain, shift, put)
        pass_y(u, q_ref.at[u])

    def feed_b(u):
        await_g(u)
        feed_backward(u, x_ref, g_ref, pool, w1, w2, gain, norms, dn_ref, put_dx(u))
        pass_dx(u)

    @pl.when(attention)
    def _():
        @pl.loop(0, UNITS)
        def _(u):
            attention_f(u)

        @pl.loop(0, UNITS)
        def _(u):
            attention_b(u)

    @pl.when(feed)
    def _():
        @pl.loop(0, 2 * UNITS)
        def _(step):
            kind = jnp.where(last, lax.rem(step, 2), lax.div(step, UNITS))
            u = jnp.where(last, lax.div(step, 2), lax.rem(step, UNITS))

            @pl.when(kind == 0)
            def _():
                feed_f(u)

            @pl.when(kind == 1)
            def _():
                feed_b(u)

    rows = UNITS * UNIT

    def attention_grad(i):
        return pltpu.make_async_copy(w1.at[:, i * 768:(i + 1) * 768], grads_hbm.at[i], gout.at[i])

    def feed_grad(i):
        if i < 4:
            src, slot = w1.at[:, i * 768:(i + 1) * 768], (6 if i == 0 else i - 1)
        else:
            src, slot = w2.at[(i - 4) * 768:(i - 3) * 768, :], (7 if i == 4 else i - 2)
        return pltpu.make_async_copy(src, grads_hbm.at[slot], gout.at[i])

    @pl.when(attention)
    def _():
        for i, (left, right) in enumerate(((n_ref, q_ref), (n_ref, k_ref), (n_ref, v_ref), (o_ref, g_ref))):
            for c in range(3):
                w1[:, i * 768 + c * 256:i * 768 + c * 256 + 256] = dot_tn(
                    left[...].reshape(rows, 768), right[:, :, c * 256:c * 256 + 256].reshape(rows, 256)).astype(BF16)
            attention_grad(i).start()

    @pl.when(feed)
    def _():
        def tile(base, t):
            slot = base + (t // 2) * UNITS
            return pool[slot:slot + UNITS, :, (t % 2) * 256:(t % 2) * 256 + 256].reshape(rows, 256)

        for i in range(4):
            for c in range(3):
                t = i * 3 + c
                w2[t * 256:t * 256 + 256, :] = dot_tn(tile(24, t), g_ref[...].reshape(rows, 768)).astype(BF16)
            feed_grad(4 + i).start()
        for i in range(4):
            for c in range(3):
                t = i * 3 + c
                w1[:, t * 256:t * 256 + 256] = dot_tn(n_ref[...].reshape(rows, 768), tile(0, t)).astype(BF16)
            feed_grad(i).start()

    norm_copy = pltpu.make_async_copy(norms, norms_hbm, load.at[0])
    norm_copy.start()

    @pl.when(attention)
    def _():
        for u in range(UNITS):
            y_store(u, y_slot(u)).wait()
        for i in range(4):
            attention_grad(i).wait()
        for i in range(2):
            lent_weight(i).wait_send()

    @pl.when(feed)
    def _():
        for u in range(UNITS):
            y_store(u, q_ref.at[u]).wait()
        for i in range(8):
            feed_grad(i).wait()

    for u in range(UNITS):
        dx_store(u).wait()

        @pl.when(jnp.logical_not(last))
        def _():
            forward_send(u, x_ref.at[u]).wait_send()

        @pl.when(jnp.logical_not(first))
        def _():
            backward_send(u).wait_send()
    norm_copy.wait()


def unit_tables(segments):
    length = segments.shape[1]
    starts = [jnp.sum((segments < v).astype(jnp.int32), axis=1, keepdims=True) for v in range(5)]
    big = jnp.full_like(starts[0], 0)
    for v in reversed(range(4)):
        big = jnp.where(starts[v + 1] - starts[v] == UNIT, starts[v], big)
    places = lax.broadcasted_iota(jnp.int32, segments.shape, 1) + big
    places = jnp.where(places >= length, places - length, places)
    gene = sum((places >= starts[v]).astype(jnp.int32) for v in (1, 2, 3))
    begin = jnp.zeros_like(places)
    for v in (1, 2, 3):
        begin = jnp.where(gene == v, starts[v], begin)
    offsets = (places - begin).astype(F32).reshape(-1, UNIT)
    lane = jnp.arange(128, dtype=jnp.int32)
    frequency = jnp.power(10000.0, -2.0 * (lane % 32).astype(F32) / HEAD_DIM)
    angles = offsets[:, :, None] * frequency
    sign = jnp.where(lane % HEAD_DIM < HEAD_DIM // 2, -1.0, 1.0)
    return big[:, 0], gene.astype(F32).reshape(-1, UNIT), jnp.cos(angles), jnp.sin(angles) * sign


def rolled(rows, first):
    length = rows.shape[1]
    return jnp.stack([
        lax.dynamic_slice_in_dim(jnp.concatenate([rows[r], rows[r]]), first[r], length, 0) for r in range(rows.shape[0])
    ])


def on_device(inputs, blocks, norm_gain, norm_bias, segments, cotangent):
    sections = lax.axis_size("section")
    parity = lax.axis_index("section") % 2
    batches, length, width = inputs.shape
    big, gene, cos, sin = unit_tables(segments)
    units = (UNITS, UNIT, width)
    x_units = rolled(inputs, big).reshape(units)
    cot_units = rolled(cotangent, big).reshape(units)
    low = lambda *shape: pltpu.VMEM(shape, BF16)
    full = lambda *shape: pltpu.VMEM(shape, F32)
    dma = lambda n: pltpu.SemaphoreType.DMA((n,))
    hbm = pl.BlockSpec(memory_space=pl.ANY)
    y, dx, grads, norms = pl.pallas_call(
        functools.partial(relay_kernel, sections),
        out_shape=(
            jax.ShapeDtypeStruct(units, BF16),
            jax.ShapeDtypeStruct(units, BF16),
            jax.ShapeDtypeStruct((8, width, width), BF16),
            jax.ShapeDtypeStruct((2, width), F32),
        ),
        in_specs=[hbm] * 9,
        out_specs=(hbm,) * 4,
        scratch_shapes=[
            *[low(*units) for _ in range(7)],
            low(48, UNIT, CHUNK), low(width, 4 * width), low(4 * width, width),
            full(UNITS, UNIT, 128), full(UNITS, UNIT, 128), full(UNITS, UNIT, 1), full(UNITS, 1, UNIT),
            full(UNIT, UNIT), low(UNIT, width), full(UNIT, width),
            full(1, width), full(1, width), full(2, width),
            dma(4), dma(4), dma(4), dma(4), dma(2), dma(2), dma(6), dma(6), dma(4), dma(4), dma(8),
        ],
        compiler_params=pltpu.CompilerParams(
            collective_id=1, has_side_effects=True, vmem_limit_bytes=64 * 2**20 - 8192),
        name="relay",
    )(x_units, cot_units, blocks[0], norm_gain, norm_bias, cos, sin, gene[:, :, None], gene[:, None, :])
    back = length - big
    back = jnp.where(back == length, 0, back)
    produced = rolled(y.reshape(inputs.shape), back)
    input_grads = rolled(dx.reshape(inputs.shape), back)
    returned = lax.ppermute(grads[6:8], "section", [(i, i - 1) for i in range(1, sections)])
    own = jnp.where(parity == 0, jnp.concatenate([grads[0:4], returned]), grads[0:6])
    summed_blocks = lax.psum_scatter(own, "dp", scatter_dimension=1, tiled=True).astype(F32)
    summed_norms = lax.psum_scatter(norms, "dp", scatter_dimension=1, tiled=True)
    return produced[None], input_grads[None], summed_blocks[None], summed_norms[0:1], summed_norms[1:2]


def solution(mesh):
    return jax.shard_map(
        on_device,
        mesh=mesh,
        in_specs=(
            P("dp", None, None),
            P("section", None, None, None),
            P("section", None),
            P("section", None),
            P("dp", None),
            P("dp", None, None),
        ),
        out_specs=(
            P("section", "dp", None, None),
            P("section", "dp", None, None),
            P("section", None, "dp", None),
            P("section", "dp"),
            P("section", "dp"),
        ),
        check_vma=False,
    )
```

```python
import functools
import jax
import jax.numpy as jnp
from jax import lax
from jax.experimental import pallas as pl
from jax.experimental.pallas import tpu as pltpu
from jax.sharding import PartitionSpec as P

HEAD_DIM = 64
EPSILON = 1e-05
MASKED = -1e30
F32 = jnp.float32
BF16 = jnp.bfloat16
CHUNK = 512
UNIT = 448
UNITS = 4
MESH = pl.DeviceIdType.MESH


def dot_nn(a, b):
    return lax.dot_general(a, b, (((1,), (0,)), ((), ())), preferred_element_type=F32)


def dot_nt(a, b):
    return lax.dot_general(a, b, (((1,), (1,)), ((), ())), preferred_element_type=F32)


def dot_tn(a, b):
    return lax.dot_general(a, b, (((0,), (0,)), ((), ())), preferred_element_type=F32)


def normed_rows(x):
    mean = jnp.mean(x, axis=-1, keepdims=True)
    centred = x - mean
    scale = lax.rsqrt(jnp.mean(centred * centred, axis=-1, keepdims=True) + EPSILON)
    return centred * scale, scale


def norm_forward(x, gain, shift):
    xhat, _ = normed_rows(x)
    return (xhat * gain + shift).astype(BF16)


def norm_backward(x, dn, gain):
    xhat, scale = normed_rows(x)
    e = dn * gain
    mean_e = jnp.mean(e, axis=-1, keepdims=True)
    mean_ex = jnp.mean(e * xhat, axis=-1, keepdims=True)
    dx = (e - mean_e - xhat * mean_ex) * scale
    return dx, jnp.sum(dn * xhat, axis=0, keepdims=True), jnp.sum(dn, axis=0, keepdims=True)


def gelu_pair(x):
    half_square = (x * x) * (-0.5 * 1.4426950408889634)
    e = jnp.exp2(half_square)
    t = 1.0 / (1.0 + (0.3275911 * 0.7071067811865476) * jnp.abs(x))
    poly = ((((1.061405429 * t - 1.453152027) * t + 1.421413741) * t - 0.284496736) * t + 0.254829592) * t
    tail = 0.5 * poly * e
    cdf = jnp.where(x < 0, tail, 1.0 - tail)
    return x * cdf, cdf + x * e * 0.3989422804014327


def turned(u):
    lane = lax.broadcasted_iota(jnp.int32, u.shape, 1)
    first = lax.rem(lane, HEAD_DIM) < HEAD_DIM // 2
    return jnp.where(first, pltpu.roll(u, 128 - 32, 1), pltpu.roll(u, 32, 1))


def feed_forward(u, x_ref, n_ref, pool, w1, w2, gain, shift, put):
    x = x_ref[u].astype(F32)
    n_ref[u] = norm_forward(x, gain[...], shift[...])

    @pl.loop(0, 6)
    def _(j):
        cols = pl.ds(pl.multiple_of(j * CHUNK, CHUNK), CHUNK)
        a0 = dot_nn(n_ref[u], w1[:, cols])
        a, slope = gelu_pair(a0)
        pool[j * 4 + u] = slope.astype(BF16)
        pool[24 + j * 4 + u] = a.astype(BF16)

    for c in range(3):
        cols = slice(c * 256, c * 256 + 256)
        a = jnp.concatenate([pool[24 + j * 4 + u] for j in range(6)], axis=1)
        put(c, cols, (x_ref[u, :, cols].astype(F32) + dot_nn(a, w2[:, cols])).astype(BF16))


def feed_backward(u, x_ref, g_ref, pool, w1, w2, gain, norms, dn_ref, put):
    @pl.loop(0, 6)
    def _(j):
        rows = pl.ds(pl.multiple_of(j * CHUNK, CHUNK), CHUNK)
        da = dot_nt(g_ref[u], w2[rows, :])
        slot = j * 4 + u
        pool[slot] = (da * pool[slot].astype(F32)).astype(BF16)

    for c in range(3):
        rows = slice(c * 256, c * 256 + 256)
        da0 = jnp.concatenate([pool[j * 4 + u] for j in range(6)], axis=1)
        dn_ref[:, rows] = dot_nt(da0, w1[rows, :])
    finish_backward(u, x_ref, g_ref, gain, norms, dn_ref, put)


def finish_backward(u, x_ref, g_ref, gain, norms, dn_ref, put):
    dx, grad_gain, grad_shift = norm_backward(x_ref[u].astype(F32), dn_ref[...], gain[...])
    norms[0, 0:1, :] += grad_gain
    norms[0, 1:2, :] += grad_shift
    put((g_ref[u].astype(F32) + dx).astype(BF16))


def part(kind, u):
    return pl.ds(pl.multiple_of((kind * UNITS + u) * UNIT, 16), UNIT)


def attention_forward(u, x_ref, n_ref, flat, pool, w1, cos_ref, sin_ref, bias_ref, gain, shift, put):
    x = x_ref[u].astype(F32)
    n_ref[u] = norm_forward(x, gain[...], shift[...])
    for kind in range(2):
        for t in range(3):
            u2 = dot_nn(n_ref[u], w1[:, kind * 768 + t * 256: kind * 768 + t * 256 + 256])
            for s in range(2):
                w = u2[:, s * 128: s * 128 + 128]
                flat[part(kind, u), t * 256 + s * 128: t * 256 + s * 128 + 128] = (w * cos_ref[u] + turned(w) * sin_ref[u]).astype(BF16)
    flat[part(2, u), :] = dot_nn(n_ref[u], w1[:, 1536:2304]).astype(BF16)

    @pl.loop(0, 6)
    def _(p):
        cols = pl.ds(pl.multiple_of(p * 128, 128), 128)
        q, k, v = (flat[part(kind, u), cols] for kind in range(3))
        low = lax.broadcasted_iota(jnp.int32, q.shape, 1) < HEAD_DIM
        outs = []
        for h in range(2):
            mine = low if h == 0 else jnp.logical_not(low)
            scores = dot_nt(jnp.where(mine, q, jnp.zeros_like(q)) * BF16(0.125), k) + bias_ref[...]
            raised = jnp.exp(scores - jnp.max(scores, axis=-1, keepdims=True))
            weights = (raised * (1.0 / jnp.sum(raised, axis=-1, keepdims=True))).astype(BF16)
            pool[u * 12 + p * 2 + h, :, 0:448] = weights
            outs.append(dot_nn(weights, v))
        flat[part(3, u), cols] = jnp.where(low, outs[0], outs[1]).astype(BF16)

    for c in range(3):
        cols = slice(c * 256, c * 256 + 256)
        put(c, cols, (x_ref[u, :, cols].astype(F32) + dot_nn(flat[part(3, u), :], w1[:, 2304 + c * 256: 2560 + c * 256])).astype(BF16))


def attention_backward(u, x_ref, g_ref, flat, pool, w1, cos_ref, sin_ref, do_ref, gain, norms, dn_ref, put):
    do_ref[...] = dot_nt(g_ref[u], w1[:, 2304:3072]).astype(BF16)

    @pl.loop(0, 6)
    def _(p):
        cols = pl.ds(pl.multiple_of(p * 128, 128), 128)
        q, k, v, o = (flat[part(kind, u), cols] for kind in range(4))
        do = do_ref[:, cols]
        low = lax.broadcasted_iota(jnp.int32, q.shape, 1) < HEAD_DIM
        dqs, dks, dvs = [], [], []
        for h in range(2):
            mine = low if h == 0 else jnp.logical_not(low)
            do8 = jnp.where(mine, do, jnp.zeros_like(do)) * BF16(0.125)
            delta = jnp.sum(do8.astype(F32) * o.astype(F32), axis=-1, keepdims=True)
            weights = pool[u * 12 + p * 2 + h, :, 0:448]
            ds = (weights.astype(F32) * (dot_nt(do8, v) - delta)).astype(BF16)
            dqs.append(dot_nn(ds, k))
            dks.append(dot_tn(ds, q))
            dvs.append(dot_tn(weights, do))
        cos, sin = cos_ref[u], sin_ref[u]
        dq = jnp.where(low, dqs[0], dqs[1])
        dk = jnp.where(low, dks[0], dks[1])
        flat[part(0, u), cols] = (dq * cos - turned(dq) * sin).astype(BF16)
        flat[part(1, u), cols] = (dk * cos - turned(dk) * sin).astype(BF16)
        flat[part(2, u), cols] = jnp.where(low, dvs[0], dvs[1]).astype(BF16)

    for c in range(3):
        rows = slice(c * 256, c * 256 + 256)
        dqkv = jnp.concatenate([flat[part(kind, u), :] for kind in range(3)], axis=1)
        dn_ref[:, rows] = dot_nt(dqkv, w1[rows, 0:2304])
    finish_backward(u, x_ref, g_ref, gain, norms, dn_ref, put)


def relay_kernel(
    sections, line_size, reduced, x_hbm, cot_hbm, blocks_hbm, gain_hbm, shift_hbm, cos_hbm, sin_hbm, segc_hbm, segr_hbm,
    y_hbm, dx_hbm, grads_hbm, norms_hbm,
    x_ref, n_ref, g_ref, flat, pool, w1, w2, cos_ref, sin_ref, segc, segr, bias, do_ref, dn_ref,
    gain, shift, norms, norms_in,
    fsend, frecv, bsend, brecv, lsend, lrecv, load, wload, yout, dxout, gout, gsend, grecv, rsend, rrecv, nsend, nrecv, ready,
):
    me = lax.axis_index("section")
    line = lax.axis_index("dp")
    ahead, behind = lax.rem(me + 1, sections), lax.rem(me + sections - 1, sections)
    first, last = me == 0, me == sections - 1
    attention = lax.rem(me, 2) == 0
    feed = jnp.logical_not(attention)

    barrier = pltpu.get_barrier_semaphore()
    bits = line_size.bit_length() - 1
    partners = [(me, line ^ (1 << bit)) for bit in range(bits)]
    for other in [(ahead, line), (behind, line)] + partners:
        pl.semaphore_signal(barrier, inc=1, device_id=other, device_id_type=MESH)

    small = [
        pltpu.make_async_copy(src, dst, load.at[i])
        for i, (src, dst) in enumerate(((gain_hbm, gain), (shift_hbm, shift)))
    ]
    tables = [
        pltpu.make_async_copy(src, dst, load.at[2 + i])
        for i, (src, dst) in enumerate(((cos_hbm, cos_ref), (sin_hbm, sin_ref), (segc_hbm, segc), (segr_hbm, segr)))
    ]

    def x_load(u):
        return pltpu.make_async_copy(x_hbm.at[u], x_ref.at[u], frecv.at[u])

    def g_load(u):
        return pltpu.make_async_copy(cot_hbm.at[u], g_ref.at[u], brecv.at[u])

    def attention_weight(i):
        return pltpu.make_async_copy(blocks_hbm.at[i], w1.at[:, i * 768:(i + 1) * 768], wload.at[i])

    def feed_weight(i):
        dst = w1.at[:, (i + 1) * 768:(i + 2) * 768] if i < 3 else w2.at[(i - 2) * 768:(i - 1) * 768, :]
        return pltpu.make_async_copy(blocks_hbm.at[i], dst, wload.at[i])

    def lent_weight(i):
        dst = w1.at[:, 0:768] if i == 0 else w2.at[0:768, :]
        return pltpu.make_async_remote_copy(
            src_ref=blocks_hbm.at[4 + i], dst_ref=dst, send_sem=lsend.at[i], recv_sem=lrecv.at[i],
            device_id=(ahead, line), device_id_type=MESH)

    def forward_send(u, src):
        return pltpu.make_async_remote_copy(
            src_ref=src, dst_ref=x_ref.at[u], send_sem=fsend.at[u], recv_sem=frecv.at[u],
            device_id=(ahead, line), device_id_type=MESH)

    def backward_send(u):
        return pltpu.make_async_remote_copy(
            src_ref=x_ref.at[u], dst_ref=g_ref.at[u], send_sem=bsend.at[u], recv_sem=brecv.at[u],
            device_id=(behind, line), device_id_type=MESH)

    def y_store(u, src):
        return pltpu.make_async_copy(src, y_hbm.at[u], yout.at[u])

    def dx_store(u):
        return pltpu.make_async_copy(x_ref.at[u], dx_hbm.at[u], dxout.at[u])

    @pl.when(first)
    def _():
        x_load(0).start()

    for copy in small:
        copy.start()

    @pl.when(attention)
    def _():
        for i in range(4):
            attention_weight(i).start()
        for copy in tables:
            copy.start()

    @pl.when(feed)
    def _():
        for i in range(6):
            feed_weight(i).start()

    @pl.when(first)
    def _():
        for u in range(1, UNITS):
            x_load(u).start()

    @pl.when(last)
    def _():
        for u in range(UNITS):
            g_load(u).start()

    pl.semaphore_wait(barrier, 2 + bits)

    @pl.when(attention)
    def _():
        for i in range(2):
            lent_weight(i).start()

    norms[0] = jnp.zeros(norms.shape[1:], F32)
    for copy in small:
        copy.wait()

    @pl.when(attention)
    def _():
        for copy in tables:
            copy.wait()
        for i in range(4):
            attention_weight(i).wait()

    @pl.when(feed)
    def _():
        for i in range(6):
            feed_weight(i).wait()
        for i in range(2):
            lent_weight(i).wait_recv()

    def y_slot(u):
        return w2.at[pl.ds(pl.multiple_of(u * UNIT, UNIT), UNIT), :]

    def await_x(u):
        @pl.when(first)
        def _():
            x_load(u).wait()

        @pl.when(jnp.logical_not(first))
        def _():
            forward_send(u, x_ref.at[u]).wait_recv()

    def await_g(u):
        @pl.when(last)
        def _():
            g_load(u).wait()

        @pl.when(jnp.logical_not(last))
        def _():
            backward_send(u).wait_recv()

    def pass_y(u, src):
        @pl.when(jnp.logical_not(last))
        def _():
            forward_send(u, src).start()
        y_store(u, src).start()

    def pass_dx(u):
        @pl.when(jnp.logical_not(first))
        def _():
            backward_send(u).start()
        dx_store(u).start()

    def put_dx(u):
        def put(value):
            x_ref[u] = value
        return put

    def attention_f(u):
        await_x(u)
        bias[...] = jnp.where(segc[u] == segr[u], 0.0, MASKED)

        def put(c, cols, value):
            w2[pl.ds(pl.multiple_of(u * UNIT, UNIT), UNIT), cols] = value
        attention_forward(u, x_ref, n_ref, flat, pool, w1, cos_ref, sin_ref, bias, gain, shift, put)
        pass_y(u, y_slot(u))

    def attention_b(u):
        await_g(u)
        attention_backward(u, x_ref, g_ref, flat, pool, w1, cos_ref, sin_ref, do_ref, gain, norms, dn_ref, put_dx(u))
        pass_dx(u)

    def feed_f(u):
        await_x(u)

        def put(c, cols, value):
            flat[part(0, u), cols] = value
        feed_forward(u, x_ref, n_ref, pool, w1, w2, gain, shift, put)
        pass_y(u, flat.at[part(0, u), :])

    def feed_b(u):
        await_g(u)
        feed_backward(u, x_ref, g_ref, pool, w1, w2, gain, norms, dn_ref, put_dx(u))
        pass_dx(u)

    @pl.when(attention)
    def _():
        @pl.loop(0, UNITS)
        def _(u):
            attention_f(u)

        @pl.loop(0, UNITS)
        def _(u):
            attention_b(u)

    @pl.when(feed)
    def _():
        @pl.loop(0, 2 * UNITS)
        def _(step):
            kind = jnp.where(last, lax.rem(step, 2), lax.div(step, UNITS))
            u = jnp.where(last, lax.div(step, 2), lax.rem(step, UNITS))

            @pl.when(kind == 0)
            def _():
                feed_f(u)

            @pl.when(kind == 1)
            def _():
                feed_b(u)

    rows = UNITS * UNIT

    spare = bits - reduced
    group = line >> spare
    order = list(range(reduced))

    def halves(b, step):
        base = 0
        for i in range(step):
            base += ((group >> order[i]) & 1) * (768 >> (i + 1))
        mine = (group >> order[step]) & 1
        size = 768 >> (step + 1)
        return base + (1 - mine) * size, base + mine * size, size

    def place(value):
        shards = 1 << reduced
        size = 768 // shards
        slots = [None] * shards
        for s in range(shards):
            slots[sum(((s >> bit) & 1) << (reduced - 1 - i) for i, bit in enumerate(order))] = value[s * size:(s + 1) * size]
        return jnp.concatenate(slots, axis=0)

    def feed_block(b, offset, size):
        return flat.at[pl.ds(pl.multiple_of(b * 768 + offset, 16), size), :]

    def attention_block(b, offset, size):
        return w1.at[pl.ds(pl.multiple_of(offset, 16), size), b * 768:(b + 1) * 768]

    def feed_landing(b, step):
        size = 768 >> (step + 1)
        if step == 0:
            return w2.at[b * size:(b + 1) * size, :]
        row = sum(8 * (768 >> (i + 1)) for i in range(1, step)) + b * size
        return w1.at[row % 768:row % 768 + size, row // 768 * 768:row // 768 * 768 + 768]

    def attention_landing(b, step):
        size = 768 >> (step + 1)
        row = sum(4 * (768 >> (i + 1)) for i in range(step)) + b * size
        return w2.at[row:row + size, :]

    def exchange(block, landing, b, step):
        sent, _, size = halves(b, step)
        return pltpu.make_async_remote_copy(
            src_ref=block(b, sent, size), dst_ref=landing(b, step), send_sem=gsend.at[b, step], recv_sem=grecv.at[b, step],
            device_id=(me, line ^ (1 << (spare + order[step]))), device_id_type=MESH)

    shard = 768 >> reduced

    def final(b):
        return dn_ref.at[b % 4 * shard:(b % 4 + 1) * shard, :]

    def reduce_blocks(count, block, landing, deliver):
        for turn in range(count + reduced - 1):
            for step in range(reduced):
                b = turn - step
                if b < 0 or b >= count:
                    continue
                exchange(block, landing, b, step).wait_recv()
                _, kept, size = halves(b, step)
                here = block(b, kept, size)
                total = here[...].astype(F32) + landing(b, step)[...].astype(F32)
                if step < reduced - 1:
                    here[...] = total.astype(BF16)
                    exchange(block, landing, b, step + 1).start()
                else:
                    if b >= 4:
                        deliver(b - 4).wait()
                    final(b)[...] = total
                    deliver(b).start()
        for b in range(count):
            if b >= count - 4:
                deliver(b).wait()
            for step in range(reduced):
                exchange(block, landing, b, step).wait_send()

    class Deliver:
        def __init__(self, b, slot, lent):
            self.copy = pltpu.make_async_remote_copy(
                src_ref=final(b), dst_ref=grads_hbm.at[slot], send_sem=rsend.at[slot - 4], recv_sem=rrecv.at[slot - 4],
                device_id=(behind, line), device_id_type=MESH) if lent else pltpu.make_async_copy(final(b), grads_hbm.at[slot], gout.at[b])
            self.lent = lent

        def start(self):
            self.copy.start()

        def wait(self):
            if self.lent:
                self.copy.wait_send()
            else:
                self.copy.wait()

    def attention_deliver(b):
        return Deliver(b, b, False)

    def feed_deliver(b):
        return Deliver(b, 4 + b, True) if b < 2 else Deliver(b, b - 2, False)

    def norm_exchange(bit):
        return pltpu.make_async_remote_copy(
            src_ref=norms.at[bit], dst_ref=norms_in.at[bit], send_sem=nsend.at[bit], recv_sem=nrecv.at[bit],
            device_id=partners[bit], device_id_type=MESH)

    def open_landings():
        for bit in range(spare, bits):
            pl.semaphore_signal(ready.at[bit], inc=1, device_id=partners[bit], device_id_type=MESH)

    def await_landings():
        for bit in range(spare, bits):
            pl.semaphore_wait(ready.at[bit], 1)

    @pl.when(attention)
    def _():
        for u in range(UNITS):
            y_store(u, y_slot(u)).wait()
            forward_send(u, y_slot(u)).wait_send()
        open_landings()
        for b, (left, right) in enumerate(((0, 0), (0, 1), (0, 2), (1, 3))):
            lhs = n_ref[...].reshape(rows, 768) if left == 0 else flat[3 * rows:4 * rows, :]
            for c in range(3):
                cols = slice(c * 256, c * 256 + 256)
                rhs = g_ref[:, :, cols].reshape(rows, 256) if right == 3 else flat[right * rows:(right + 1) * rows, cols]
                w1[:, b * 768 + c * 256:b * 768 + c * 256 + 256] = place(dot_tn(lhs, rhs).astype(BF16))
            if b == 0:
                await_landings()
            exchange(attention_block, attention_landing, b, 0).start()

    @pl.when(feed)
    def _():
        for u in range(UNITS):
            y_store(u, flat.at[part(0, u), :]).wait()

            @pl.when(jnp.logical_not(last))
            def _():
                forward_send(u, flat.at[part(0, u), :]).wait_send()
        open_landings()

        def tile(base, t):
            slot = base + (t // 2) * UNITS
            return pool[slot:slot + UNITS, :, (t % 2) * 256:(t % 2) * 256 + 256].reshape(rows, 256)

        for b, (second, i) in enumerate(((0, 0), (1, 0), (0, 1), (0, 2), (0, 3), (1, 1), (1, 2), (1, 3))):
            for c in range(3):
                cols = slice(c * 256, c * 256 + 256)
                if second:
                    lhs = jnp.concatenate([tile(24, i * 3 + t) for t in range(3)], axis=1)
                    value = dot_tn(lhs, g_ref[:, :, cols].reshape(rows, 256))
                else:
                    value = dot_tn(n_ref[...].reshape(rows, 768), tile(0, i * 3 + c))
                flat[b * 768:(b + 1) * 768, cols] = place(value.astype(BF16))
            if b == 0:
                await_landings()
            exchange(feed_block, feed_landing, b, 0).start()

    norm_exchange(0).start()
    for bit in range(bits):
        norm_exchange(bit).wait()
        norms[bit + 1] = norms[bit] + norms_in[bit]
        if bit + 1 < bits:
            norm_exchange(bit + 1).start()
    norm_copy = pltpu.make_async_copy(norms.at[bits], norms_hbm, load.at[0])
    norm_copy.start()

    @pl.when(attention)
    def _():
        reduce_blocks(4, attention_block, attention_landing, attention_deliver)
        for i in range(2):
            lent_weight(i).wait_send()
            feed_deliver(i).copy.wait_recv()

    @pl.when(feed)
    def _():
        reduce_blocks(8, feed_block, feed_landing, feed_deliver)

    for u in range(UNITS):
        dx_store(u).wait()

        @pl.when(jnp.logical_not(first))
        def _():
            backward_send(u).wait_send()
    norm_copy.wait()


def unit_tables(segments):
    length = segments.shape[1]
    starts = [jnp.sum((segments < v).astype(jnp.int32), axis=1, keepdims=True) for v in range(5)]
    big = jnp.full_like(starts[0], 0)
    for v in reversed(range(4)):
        big = jnp.where(starts[v + 1] - starts[v] == UNIT, starts[v], big)
    places = lax.broadcasted_iota(jnp.int32, segments.shape, 1) + big
    places = jnp.where(places >= length, places - length, places)
    gene = sum((places >= starts[v]).astype(jnp.int32) for v in (1, 2, 3))
    begin = jnp.zeros_like(places)
    for v in (1, 2, 3):
        begin = jnp.where(gene == v, starts[v], begin)
    offsets = (places - begin).astype(F32).reshape(-1, UNIT)
    lane = jnp.arange(128, dtype=jnp.int32)
    frequency = jnp.power(10000.0, -2.0 * (lane % 32).astype(F32) / HEAD_DIM)
    angles = offsets[:, :, None] * frequency
    sign = jnp.where(lane % HEAD_DIM < HEAD_DIM // 2, -1.0, 1.0)
    return big[:, 0], gene.astype(F32).reshape(-1, UNIT), jnp.cos(angles), jnp.sin(angles) * sign


def rolled(rows, first):
    length = rows.shape[1]
    return jnp.stack([
        lax.dynamic_slice_in_dim(jnp.concatenate([rows[r], rows[r]]), first[r], length, 0) for r in range(rows.shape[0])
    ])


def on_device(inputs, blocks, norm_gain, norm_bias, segments, cotangent):
    sections, line_size = lax.axis_size("section"), lax.axis_size("dp")
    bits = line_size.bit_length() - 1
    reduced = max(n for n in range(bits + 1) if (inputs.shape[2] >> n) % 16 == 0)
    batches, length, width = inputs.shape
    big, gene, cos, sin = unit_tables(segments)
    units = (UNITS, UNIT, width)
    x_units = rolled(inputs, big).reshape(units)
    cot_units = rolled(cotangent, big).reshape(units)
    low = lambda *shape: pltpu.VMEM(shape, BF16)
    full = lambda *shape: pltpu.VMEM(shape, F32)
    dma = lambda n: pltpu.SemaphoreType.DMA((n,))
    hbm = pl.BlockSpec(memory_space=pl.ANY)
    y, dx, grads, norms = pl.pallas_call(
        functools.partial(relay_kernel, sections, line_size, reduced),
        out_shape=(
            jax.ShapeDtypeStruct(units, BF16),
            jax.ShapeDtypeStruct(units, BF16),
            jax.ShapeDtypeStruct((6, width >> reduced, width), F32),
            jax.ShapeDtypeStruct((8, width), F32),
        ),
        in_specs=[hbm] * 9,
        out_specs=(hbm,) * 4,
        scratch_shapes=[
            *[low(*units) for _ in range(3)], low(4 * UNITS * UNIT, width),
            low(48, UNIT, CHUNK), low(width, 4 * width), low(4 * width, width),
            full(UNITS, UNIT, 128), full(UNITS, UNIT, 128), full(UNITS, UNIT, 1), full(UNITS, 1, UNIT),
            full(UNIT, UNIT), low(UNIT, width), full(UNIT, width),
            full(1, width), full(1, width), full(bits + 1, 8, width), full(bits, 8, width),
            dma(4), dma(4), dma(4), dma(4), dma(2), dma(2), dma(6), dma(6), dma(4), dma(4), dma(8),
            pltpu.SemaphoreType.DMA((8, reduced)), pltpu.SemaphoreType.DMA((8, reduced)), dma(2), dma(2), dma(bits), dma(bits),
            pltpu.SemaphoreType.REGULAR((bits,)),
        ],
        compiler_params=pltpu.CompilerParams(
            collective_id=1, has_side_effects=True, vmem_limit_bytes=64 * 2**20 - 8192),
        name="relay",
    )(x_units, cot_units, blocks[0], norm_gain, norm_bias, cos, sin, gene[:, :, None], gene[:, None, :])
    back = length - big
    back = jnp.where(back == length, 0, back)
    produced = rolled(y.reshape(inputs.shape), back)
    input_grads = rolled(dx.reshape(inputs.shape), back)
    if bits > reduced:
        near = 1 << (bits - reduced)
        groups = [list(range(i, i + near)) for i in range(0, line_size, near)]
        grads = lax.psum_scatter(grads, "dp", scatter_dimension=1, axis_index_groups=groups, tiled=True)
    own = width // line_size
    norms = lax.dynamic_slice_in_dim(norms, lax.axis_index("dp") * own, own, 1)
    return produced[None], input_grads[None], grads[None], norms[0:1], norms[1:2]


def solution(mesh):
    return jax.shard_map(
        on_device,
        mesh=mesh,
        in_specs=(
            P("dp", None, None),
            P("section", None, None, None),
            P("section", None),
            P("section", None),
            P("dp", None),
            P("dp", None, None),
        ),
        out_specs=(
            P("section", "dp", None, None),
            P("section", "dp", None, None),
            P("section", None, "dp", None),
            P("section", "dp"),
            P("section", "dp"),
        ),
        check_vma=False,
    )
```

```python
import functools

import jax
import jax.numpy as jnp
import ml_dtypes
import numpy as np
from jax import lax
from jax.experimental import pallas as pl
from jax.experimental.pallas import tpu as pltpu
from jax.sharding import PartitionSpec as P

HEAD_DIM = 64
EPSILON = 1e-05
MASKED = -1e30
F32 = jnp.float32
BF16 = jnp.bfloat16
CHUNK = 512
PAIRS = 6
PARTS = 3
BACK_PARTS = 4
EARLY = 2
SECOND_FIRST = (3, 6)
STEP = 3
STEP_BACK = 3
UNIT = 448
UNITS = 4
MESH = pl.DeviceIdType.MESH


def dot_nn(a, b):
    return lax.dot_general(a, b, (((1,), (0,)), ((), ())), preferred_element_type=F32)


def dot_nt(a, b):
    return lax.dot_general(a, b, (((1,), (1,)), ((), ())), preferred_element_type=F32)


def dot_tn(a, b):
    return lax.dot_general(a, b, (((0,), (0,)), ((), ())), preferred_element_type=F32)


def normed_rows(x):
    mean = jnp.mean(x, axis=-1, keepdims=True)
    centred = x - mean
    scale = lax.rsqrt(jnp.mean(centred * centred, axis=-1, keepdims=True) + EPSILON)
    return centred * scale, scale


def norm_forward(x, gain, shift):
    xhat, _ = normed_rows(x)
    return (xhat * gain + shift).astype(BF16)


def norm_backward(x, dn, gain):
    xhat, scale = normed_rows(x)
    e = dn * gain
    mean_e = jnp.mean(e, axis=-1, keepdims=True)
    mean_ex = jnp.mean(e * xhat, axis=-1, keepdims=True)
    dx = (e - mean_e - xhat * mean_ex) * scale
    return dx, jnp.sum(dn * xhat, axis=0, keepdims=True), jnp.sum(dn, axis=0, keepdims=True)


def gelu_pair(x):
    cdf = 0.5 + 0.5 * lax.erf(x * 0.7071067811865476)
    e = jnp.exp2((x * x) * (-0.5 * 1.4426950408889634))
    return x * cdf, cdf + (x * 0.3989422804014327) * e


def turned(u):
    lane = lax.broadcasted_iota(jnp.int32, u.shape, 1)
    first = lax.rem(lane, HEAD_DIM) < HEAD_DIM // 2
    return jnp.where(first, pltpu.roll(u, 128 - 32, 1), pltpu.roll(u, 32, 1))


def feed_forward(u, x_ref, n_ref, pool, w1, w2, gain, shift, put):
    x = x_ref[u].astype(F32)
    n_ref[u] = norm_forward(x, gain[...], shift[...])
    parts = []
    ahead = dot_nn(n_ref[u], w1[:, 0:CHUNK])
    for j in range(6):
        a0 = ahead
        if j < 5:
            ahead = dot_nn(n_ref[u], w1[:, (j + 1) * CHUNK:(j + 2) * CHUNK])
        a, slope = gelu_pair(a0)
        pool[j * 4 + u] = slope.astype(BF16)
        pool[24 + j * 4 + u] = a.astype(BF16)

    for c in range(3):
        cols = slice(c * 256, c * 256 + 256)
        a = jnp.concatenate([pool[24 + j * 4 + u] for j in range(6)], axis=1)
        put(c, cols, (x_ref[u, :, cols].astype(F32) + dot_nn(a, w2[:, cols])).astype(BF16))


def feed_backward(u, x_ref, g_ref, pool, w1, w2, gain, norms, dn_ref, put):
    for j in range(6):
        da = dot_nt(g_ref[u], w2[j * CHUNK:(j + 1) * CHUNK, :])
        slot = j * 4 + u
        pool[slot] = (da * pool[slot].astype(F32)).astype(BF16)

    for c in range(3):
        rows = slice(c * 256, c * 256 + 256)
        da0 = jnp.concatenate([pool[j * 4 + u] for j in range(6)], axis=1)
        dn_ref[:, rows] = dot_nt(da0, w1[rows, :])
    finish_backward(u, x_ref, g_ref, gain, norms, dn_ref, put)


def finish_backward(u, x_ref, g_ref, gain, norms, dn_ref, put):
    for i in range(BACK_PARTS):
        rows = slice(i * UNIT // BACK_PARTS, (i + 1) * UNIT // BACK_PARTS)
        dx, grad_gain, grad_shift = norm_backward(x_ref[u, rows, :].astype(F32), dn_ref[rows, :], gain[...])
        norms[0, 0:1, :] += grad_gain
        norms[0, 1:2, :] += grad_shift
        put(i, rows, (g_ref[u, rows, :].astype(F32) + dx).astype(BF16))


def part(kind, u):
    return pl.ds(pl.multiple_of((kind * UNITS + u) * UNIT, 16), UNIT)


def row_starts(segs, r):
    row = segs[r]
    count = lambda v: jnp.sum((row < v).astype(F32), axis=1, keepdims=True)
    starts = [count(v) for v in range(5)]
    big = jnp.zeros_like(starts[0])
    for v in reversed(range(4)):
        big = jnp.where(starts[v + 1] - starts[v] == UNIT, starts[v], big)
    return starts[1:4], big


def wrapped(places):
    return jnp.where(places >= 2 * UNIT, places - 2 * UNIT, places)


def iota(shape, axis):
    return lax.broadcasted_iota(jnp.int32, shape, axis).astype(F32)


def unit_places(segs, u, shape, axis):
    starts, big = row_starts(segs, lax.div(u, 2))
    place = wrapped(iota(shape, axis) + lax.rem(u, 2).astype(F32) * UNIT + big)
    gene, begin = jnp.zeros_like(place), jnp.zeros_like(place)
    for start in starts:
        gene = gene + (place >= start).astype(F32)
        begin = jnp.where(place >= start, start, begin)
    return gene, place - begin


def turn_part(rows, shift, half):
    wanted = wrapped(wrapped(iota((UNIT, 1), 0) + half * UNIT + shift))
    pick = (iota((UNIT, 2 * UNIT), 1) == wanted).astype(F32).astype(BF16)
    return dot_nn(pick, rows).astype(BF16)


def unit_tables(segs, u, table, cos_ref, sin_ref, marks):
    gene, place = unit_places(segs, u, (UNIT, 1), 0)
    lane = lax.rem(lax.broadcasted_iota(jnp.int32, (UNIT, 128), 1), HEAD_DIM).astype(F32)
    marks[0] = (lane == gene).astype(F32).astype(BF16)
    marks[1] = jnp.where(jnp.logical_and(lane < 4, lane != gene), MASKED, 0.0).astype(BF16)
    pick = (iota((UNIT, UNIT), 1) == place).astype(F32).astype(BF16)
    pieces = dot_nn(pick, table[...])
    cos_ref[u] = pieces[:, 0:128] + pieces[:, 256:384] + pieces[:, 512:640]
    sin_ref[u] = pieces[:, 128:256] + pieces[:, 384:512] + pieces[:, 640:768]


def attention_forward(u, x_ref, n_ref, flat, pool, w1, cos_ref, sin_ref, marks, scale_ref, gain, shift, put):
    x = x_ref[u].astype(F32)
    n_ref[u] = norm_forward(x, gain[...], shift[...])
    ahead = dot_nn(n_ref[u], w1[:, 0:256])
    for t in range(6):
        pair, ahead = ahead, dot_nn(n_ref[u], w1[:, (t + 1) * 256:(t + 2) * 256])
        for i in range(2):
            w = pair[:, i * 128:i * 128 + 128]
            cols = slice(t % 3 * 256 + i * 128, t % 3 * 256 + i * 128 + 128)
            flat[part(t // 3, u), cols] = (w * cos_ref[u] + turned(w) * sin_ref[u]).astype(BF16)
    flat[part(2, u), 0:256] = ahead.astype(BF16)
    flat[part(2, u), 256:768] = dot_nn(n_ref[u], w1[:, 1792:2304]).astype(BF16)

    lane = lax.broadcasted_iota(jnp.int32, (UNIT, 128), 1)
    low = lane < HEAD_DIM
    scale_ref[u] = jnp.zeros((UNIT, 128), F32)

    def heads(group):
        found = []
        for i in range(STEP):
            p = group * STEP + i
            cols = pl.ds(pl.multiple_of(p * 128, 128), 128)
            q, k, v = (flat[part(kind, u), cols] for kind in range(3))
            q = q * BF16(0.125)
            v = jnp.concatenate([v, jnp.ones_like(v)], axis=1)
            for h in range(2):
                mine = low if h == 0 else jnp.logical_not(low)
                found.append((p, h, cols, jnp.where(mine, q, marks[0]), jnp.where(mine, k, marks[1]), v))
        return found

    @pl.loop(0, PAIRS // STEP)
    def _(group):
        found = heads(group)
        scores, raised, outs = {}, {}, {}
        for t in range(len(found) + 2):
            if t < len(found):
                scores[t] = dot_nt(found[t][3], found[t][4])
            if 0 <= t - 1 < len(found):
                p, h = found[t - 1][:2]
                part_scores = scores.pop(t - 1)
                raised[t - 1] = jnp.exp(part_scores - jnp.max(part_scores, axis=-1, keepdims=True)).astype(BF16)
                pool[u * 12 + p * 2 + h, :, 0:UNIT] = raised[t - 1]
            if t - 2 >= 0:
                p, h, cols, _, _, v = found[t - 2]
                both = dot_nn(raised.pop(t - 2), v)
                scale = 1.0 / both[:, 128:256]
                scale_ref[u] = jnp.where(lane == p * 2 + h, scale, scale_ref[u])
                outs[h] = both[:, 0:128] * scale
                if h == 1:
                    flat[part(3, u), cols] = jnp.where(low, outs[0], outs[1]).astype(BF16)

    for c in range(3):
        cols = slice(c * 256, c * 256 + 256)
        put(c, cols, (x_ref[u, :, cols].astype(F32) + dot_nn(flat[part(3, u), :], w1[:, 2304 + c * 256: 2560 + c * 256])).astype(BF16))


def attention_backward(u, x_ref, g_ref, flat, pool, w1, cos_ref, sin_ref, do_ref, scale_ref, gain, norms, dn_ref, put):
    do_ref[...] = dot_nt(g_ref[u], w1[:, 2304:3072]).astype(BF16)

    lane = lax.broadcasted_iota(jnp.int32, (UNIT, 128), 1)
    low = lane < HEAD_DIM

    def pairs(group):
        found = []
        for i in range(STEP_BACK):
            p = group * STEP_BACK + i
            cols = pl.ds(pl.multiple_of(p * 128, 128), 128)
            q, k, v, o = (flat[part(kind, u), cols] for kind in range(4))
            scales = [jnp.sum(jnp.where(lane == p * 2 + h, scale_ref[u], 0.0), axis=-1, keepdims=True) for h in range(2)]
            do = (do_ref[:, cols].astype(F32) * jnp.where(low, scales[0], scales[1])).astype(BF16)
            inner = do.astype(F32) * o.astype(F32) * 0.125
            for h in range(2):
                mine = low if h == 0 else jnp.logical_not(low)
                delta = jnp.sum(jnp.where(mine, inner, 0.0), axis=-1, keepdims=True)
                found.append((p, h, cols, q, k, v, do, jnp.where(mine, do, jnp.zeros_like(do)) * BF16(0.125), delta))
        return found

    @pl.loop(0, PAIRS // STEP_BACK)
    def _(group):
        found = pairs(group)
        slopes, ready, kept = {}, {}, {}
        for t in range(len(found) + 2):
            if t < len(found):
                slopes[t] = dot_nt(found[t][7], found[t][5])
            if 0 <= t - 1 < len(found):
                p, h = found[t - 1][:2]
                raised = pool[u * 12 + p * 2 + h, :, 0:UNIT]
                ready[t - 1] = raised * (slopes.pop(t - 1) - found[t - 1][8]).astype(BF16), raised
            if t - 2 >= 0:
                p, h, cols, q, k, v, do = found[t - 2][:7]
                ds, raised = ready.pop(t - 2)
                kept[h] = dot_nn(ds, k), dot_tn(ds, q), dot_tn(raised, do)
                if h == 1:
                    cos, sin = cos_ref[u], sin_ref[u]
                    dq, dk, dv = (jnp.where(low, kept[0][i], kept[1][i]) for i in range(3))
                    flat[part(0, u), cols] = (dq * cos - turned(dq) * sin).astype(BF16)
                    flat[part(1, u), cols] = (dk * cos - turned(dk) * sin).astype(BF16)
                    flat[part(2, u), cols] = dv.astype(BF16)

    for c in range(3):
        rows = slice(c * 256, c * 256 + 256)
        dqkv = jnp.concatenate([flat[part(kind, u), :] for kind in range(3)], axis=1)
        dn_ref[:, rows] = dot_nt(dqkv, w1[rows, 0:2304])
    finish_backward(u, x_ref, g_ref, gain, norms, dn_ref, put)


def relay_kernel(
    sections, line_size, reduced, x_hbm, cot_hbm, blocks_hbm, gain_hbm, shift_hbm, segs_hbm, table_hbm,
    y_hbm, dx_hbm, grads_hbm, norms_hbm,
    x_ref, n_ref, g_ref, flat, pool, w1, w2, cos_ref, sin_ref, segs, table, marks, scale_ref, do_ref, dn_ref, rowbuf,
    gain, shift, norms, norms_in,
    fsend, frecv, bsend, brecv, lsend, lrecv, load, wload, yout, gout, gsend, grecv, rsend, rrecv, nsend, nrecv, ready,
):
    me = lax.axis_index("section")
    line = lax.axis_index("dp")
    ahead, behind = lax.rem(me + 1, sections), lax.rem(me + sections - 1, sections)
    first, last = me == 0, me == sections - 1
    attention = lax.rem(me, 2) == 0
    feed = jnp.logical_not(attention)

    barrier = pltpu.get_barrier_semaphore()
    bits = line_size.bit_length() - 1
    partners = [(me, line ^ (1 << bit)) for bit in range(bits)]
    for other in [(ahead, line), (behind, line)] + partners:
        pl.semaphore_signal(barrier, inc=1, device_id=other, device_id_type=MESH)

    small = [
        pltpu.make_async_copy(src, dst, load.at[i])
        for i, (src, dst) in enumerate(((gain_hbm, gain), (shift_hbm, shift), (segs_hbm, segs)))
    ]
    table_load = pltpu.make_async_copy(table_hbm, table, load.at[3])

    def row_load(src, r):
        return pltpu.make_async_copy(src.at[r], rowbuf, load.at[4])

    def turn_in(src, r, dst):
        row_load(src, r).wait()
        _, big = row_starts(segs, r)
        for half in range(2):
            for c in range(3):
                cols = slice(c * 256, c * 256 + 256)
                dst[2 * r + half, :, cols] = turn_part(rowbuf[:, cols], big, half)

    def row_store(dst, r):
        return pltpu.make_async_copy(rowbuf, dst.at[r], yout)

    def turn_out(read, r, dst):
        _, big = row_starts(segs, r)
        for half in range(2):
            for c in range(3):
                cols = slice(c * 256, c * 256 + 256)
                both = jnp.concatenate([read(2 * r, cols), read(2 * r + 1, cols)], axis=0)
                rowbuf[half * UNIT:(half + 1) * UNIT, cols] = turn_part(both, 2 * UNIT - big, half)
        row_store(dst, r).start()

    def attention_weight(i):
        return pltpu.make_async_copy(blocks_hbm.at[i], w1.at[:, i * 768:(i + 1) * 768], wload.at[i])

    def feed_weight(i):
        dst = w1.at[:, (i + 1) * 768:(i + 2) * 768] if i < 3 else w2.at[(i - 2) * 768:(i - 1) * 768, :]
        return pltpu.make_async_copy(blocks_hbm.at[i], dst, wload.at[i])

    def lent_weight(i):
        dst = w1.at[:, 0:768] if i == 0 else w2.at[0:768, :]
        return pltpu.make_async_remote_copy(
            src_ref=blocks_hbm.at[4 + i], dst_ref=dst, send_sem=lsend.at[i], recv_sem=lrecv.at[i],
            device_id=(ahead, line), device_id_type=MESH)

    def forward_send(buffer, u, c):
        cols = slice(c * 256, c * 256 + 256)
        return pltpu.make_async_remote_copy(
            src_ref=buffer.at[part(0, u), cols], dst_ref=x_ref.at[u, :, cols], send_sem=fsend.at[u, c], recv_sem=frecv.at[u, c],
            device_id=(ahead, line), device_id_type=MESH)

    def backward_send(u, i):
        rows = slice(i * UNIT // BACK_PARTS, (i + 1) * UNIT // BACK_PARTS)
        return pltpu.make_async_remote_copy(
            src_ref=x_ref.at[u, rows, :], dst_ref=g_ref.at[u, rows, :], send_sem=bsend.at[u, i], recv_sem=brecv.at[u, i],
            device_id=(behind, line), device_id_type=MESH)

    @pl.when(first)
    def _():
        row_load(x_hbm, 0).start()

    @pl.when(last)
    def _():
        row_load(cot_hbm, 0).start()

    for copy in small:
        copy.start()

    @pl.when(attention)
    def _():
        for i in range(4):
            attention_weight(i).start()
        table_load.start()

    @pl.when(feed)
    def _():
        for i in range(6):
            feed_weight(i).start()

    pl.semaphore_wait(barrier, 2 + bits)

    @pl.when(attention)
    def _():
        for i in range(2):
            lent_weight(i).start()

    norms[0] = jnp.zeros(norms.shape[1:], F32)
    for copy in small:
        copy.wait()

    @pl.when(first)
    def _():
        turn_in(x_hbm, 0, x_ref)
        row_load(x_hbm, 1).start()

    @pl.when(attention)
    def _():
        table_load.wait()
        for i in range(4):
            attention_weight(i).wait()

    @pl.when(feed)
    def _():
        for i in range(6):
            feed_weight(i).wait()
        for i in range(2):
            lent_weight(i).wait_recv()

    def await_x(u):
        @pl.when(jnp.logical_not(first))
        def _():
            for c in range(PARTS):
                forward_send(flat, u, c).wait_recv()

    def await_g(u):
        @pl.when(jnp.logical_not(last))
        def _():
            for i in range(BACK_PARTS):
                backward_send(u, i).wait_recv()

    def put_y(buffer, u):
        def put(c, cols, value):
            buffer[part(0, u), cols] = value

            @pl.when(jnp.logical_not(last))
            def _():
                forward_send(buffer, u, c).start()
        return put

    def put_dx(u):
        def put(i, rows, value):
            x_ref[u, rows, :] = value

            @pl.when(jnp.logical_not(first))
            def _():
                backward_send(u, i).start()
        return put

    def y_part(read):
        for r in range(2):
            turn_out(read, r, y_hbm)
            row_store(y_hbm, r).wait()

    def read_x(u, cols):
        return x_ref[u, :, cols]

    def attention_f(u):
        unit_tables(segs, u, table, cos_ref, sin_ref, marks)
        await_x(u)
        attention_forward(u, x_ref, n_ref, flat, pool, w1, cos_ref, sin_ref, marks, scale_ref, gain, shift, put_y(w2, u))

    def attention_b(u):
        await_g(u)
        attention_backward(u, x_ref, g_ref, flat, pool, w1, cos_ref, sin_ref, do_ref, scale_ref, gain, norms, dn_ref, put_dx(u))

    def feed_f(u):
        await_x(u)
        feed_forward(u, x_ref, n_ref, pool, w1, w2, gain, shift, put_y(flat, u))

    def feed_b(u):
        @pl.when(u < UNITS - 1)
        def _():
            await_g(u)
        feed_backward(u, x_ref, g_ref, pool, w1, w2, gain, norms, dn_ref, put_dx(u))

    rows = UNITS * UNIT

    spare = bits - reduced
    group = line >> spare
    first_bit = list(range(reduced))
    second_bit = [1, 0] + list(range(2, reduced)) if reduced > 1 else first_bit

    def order_of(b):
        return second_bit if b in SECOND_FIRST else first_bit

    def halves(b, step):
        base, order = 0, order_of(b)
        for i in range(step):
            base += ((group >> order[i]) & 1) * (768 >> (i + 1))
        mine = (group >> order[step]) & 1
        size = 768 >> (step + 1)
        return base + (1 - mine) * size, base + mine * size, size

    def place(value, b):
        order = order_of(b)
        shards = 1 << reduced
        size = 768 // shards
        slots = [None] * shards
        for s in range(shards):
            slots[sum(((s >> bit) & 1) << (reduced - 1 - i) for i, bit in enumerate(order))] = value[s * size:(s + 1) * size]
        return jnp.concatenate(slots, axis=0)

    def feed_block(b, offset, size):
        return flat.at[pl.ds(pl.multiple_of(b * 768 + offset, 16), size), :]

    def attention_block(b, offset, size):
        return w1.at[pl.ds(pl.multiple_of(offset, 16), size), b * 768:(b + 1) * 768]

    def feed_landing(b, step):
        size = 768 >> (step + 1)
        if step == 0 and b < EARLY:
            return flat.at[8 * 768 + b * size:8 * 768 + (b + 1) * size, :]
        if step == 0:
            return w2.at[b * size:(b + 1) * size, :]
        row = sum(8 * (768 >> (i + 1)) for i in range(1, step)) + b * size
        return w1.at[row % 768:row % 768 + size, row // 768 * 768:row // 768 * 768 + 768]

    def attention_landing(b, step):
        size = 768 >> (step + 1)
        row = sum(4 * (768 >> (i + 1)) for i in range(step)) + b * size
        return w2.at[row:row + size, :]

    def exchange(block, landing, b, step):
        sent, _, size = halves(b, step)
        return pltpu.make_async_remote_copy(
            src_ref=block(b, sent, size), dst_ref=landing(b, step), send_sem=gsend.at[b, step], recv_sem=grecv.at[b, step],
            device_id=(me, line ^ (1 << (spare + order_of(b)[step]))), device_id_type=MESH)

    shard = 768 >> reduced

    def final(b):
        return dn_ref.at[b % 4 * shard:(b % 4 + 1) * shard, :]

    def reduce_blocks(count, early, grad, block, landing, deliver):
        ahead_by = 2
        for turn in range(-ahead_by, count + reduced - 1):
            fresh = turn + ahead_by
            if fresh < count and fresh >= early:
                grad(fresh)
                if fresh == early:
                    await_landings()
                if turn < 0:
                    exchange(block, landing, fresh, 0).start()
            for step in range(reduced):
                b = turn - step
                if b < 0 or b >= count:
                    continue
                exchange(block, landing, b, step).wait_recv()
                if step == 0 and fresh < count:
                    exchange(block, landing, fresh, 0).start()
                _, kept, size = halves(b, step)
                here = block(b, kept, size)
                total = here[...].astype(F32) + landing(b, step)[...].astype(F32)
                if step < reduced - 1:
                    here[...] = total.astype(BF16)
                    exchange(block, landing, b, step + 1).start()
                else:
                    if b >= 4:
                        deliver(b - 4).wait()
                    final(b)[...] = total
                    deliver(b).start()
            if turn in (0, 1):
                if turn == 1:
                    row_store(dx_hbm, 0).wait()
                turn_out(read_x, turn, dx_hbm)
            bit = turn + ahead_by - 1
            if 0 <= bit < bits:
                norm_step(bit)
        for b in range(count):
            if b >= count - 4:
                deliver(b).wait()
            for step in range(reduced):
                exchange(block, landing, b, step).wait_send()
        row_store(dx_hbm, 1).wait()

    class Deliver:
        def __init__(self, b, slot, lent):
            self.copy = pltpu.make_async_remote_copy(
                src_ref=final(b), dst_ref=grads_hbm.at[slot], send_sem=rsend.at[slot - 4], recv_sem=rrecv.at[slot - 4],
                device_id=(behind, line), device_id_type=MESH) if lent else pltpu.make_async_copy(final(b), grads_hbm.at[slot], gout.at[b])
            self.lent = lent

        def start(self):
            self.copy.start()

        def wait(self):
            if self.lent:
                self.copy.wait_send()
            else:
                self.copy.wait()

    def attention_deliver(b):
        return Deliver(b, b, False)

    def feed_deliver(b):
        slot, lent = ((5, True), (3, False), (4, True), (0, False), (1, False), (2, False), (4, False), (5, False))[b]
        return Deliver(b, slot, lent)

    def norm_exchange(bit):
        return pltpu.make_async_remote_copy(
            src_ref=norms.at[bit], dst_ref=norms_in.at[bit], send_sem=nsend.at[bit], recv_sem=nrecv.at[bit],
            device_id=partners[bit], device_id_type=MESH)

    def norm_step(bit):
        if bit == 0:
            norm_exchange(0).start()
        norm_exchange(bit).wait()
        norms[bit + 1] = norms[bit] + norms_in[bit]
        if bit + 1 < bits:
            norm_exchange(bit + 1).start()
        else:
            norm_copy.start()

    norm_copy = pltpu.make_async_copy(norms.at[bits], norms_hbm, load.at[0])

    def open_landings():
        for bit in range(spare, bits):
            pl.semaphore_signal(ready.at[bit], inc=1, device_id=partners[bit], device_id_type=MESH)

    def await_landings():
        for bit in range(spare, bits):
            pl.semaphore_wait(ready.at[bit], 1)

    def attention_grad(b):
        lhs = n_ref[...].reshape(rows, 768) if b < 3 else flat[3 * rows:4 * rows, :]
        for c in range(3):
            cols = slice(c * 256, c * 256 + 256)
            rhs = flat[b * rows:(b + 1) * rows, cols] if b < 3 else g_ref[:, :, cols].reshape(rows, 256)
            w1[:, b * 768 + c * 256:b * 768 + c * 256 + 256] = place(dot_tn(lhs, rhs).astype(BF16), b)

    def tile(base, t):
        slot = base + (t // 2) * UNITS
        return pool[slot:slot + UNITS, :, (t % 2) * 256:(t % 2) * 256 + 256].reshape(rows, 256)

    def feed_grad(b):
        second, i = ((1, 0), (1, 1), (0, 0), (0, 1), (0, 2), (0, 3), (1, 2), (1, 3))[b]
        for c in range(3):
            cols = slice(c * 256, c * 256 + 256)
            if second:
                lhs = jnp.concatenate([tile(24, i * 3 + t) for t in range(3)], axis=1)
                value = dot_tn(lhs, g_ref[:, :, cols].reshape(rows, 256))
            else:
                value = dot_tn(n_ref[...].reshape(rows, 768), tile(0, i * 3 + c))
            flat[b * 768:(b + 1) * 768, cols] = place(value.astype(BF16), b)

    @pl.when(attention)
    def _():
        for r in range(2):
            if r == 1:
                @pl.when(first)
                def _():
                    turn_in(x_hbm, 1, x_ref)

            @pl.loop(2 * r, 2 * r + 2)
            def _(u):
                attention_f(u)

        @pl.loop(0, 2)
        def _(phase):
            @pl.when(phase == jnp.where(first, 0, 1))
            def _():
                y_part(lambda u, cols: w2[part(0, u), cols])

            @pl.when(phase == 0)
            def _():
                @pl.loop(0, UNITS)
                def _(u):
                    attention_b(u)

    @pl.when(feed)
    def _():
        @pl.when(last)
        def _():
            turn_in(cot_hbm, 0, g_ref)
            row_load(cot_hbm, 1).start()
            turn_in(cot_hbm, 1, g_ref)

        def early_grads():
            await_g(UNITS - 1)

            @pl.when(jnp.logical_not(last))
            def _():
                for u in range(UNITS):
                    for c in range(PARTS):
                        forward_send(flat, u, c).wait_send()
            for b in range(EARLY):
                feed_grad(b)
                exchange(feed_block, feed_landing, b, 0).start()

        forward, backward, output, grads = range(4)

        @pl.loop(0, 2 * UNITS + 2)
        def _(step):
            over = step >= 2 * UNITS
            relay = step - UNITS - 1
            kind = jnp.where(
                last,
                jnp.where(over, step - 2 * UNITS + output, lax.rem(step, 2)),
                jnp.where(step < UNITS, forward, jnp.where(relay < 0, output, jnp.where(relay == UNITS - 1, grads, backward))))
            u = jnp.where(last, jnp.where(over, 0, lax.div(step, 2)), jnp.where(step < UNITS, step, jnp.minimum(jnp.maximum(relay, 0), UNITS - 1)))

            @pl.when(kind == forward)
            def _():
                feed_f(u)

            @pl.when(kind == backward)
            def _():
                feed_b(u)

            @pl.when(kind == output)
            def _():
                y_part(lambda v, cols: flat[part(0, v), cols])

            @pl.when(kind == grads)
            def _():
                early_grads()

    @pl.when(attention)
    def _():
        for u in range(UNITS):
            for c in range(PARTS):
                forward_send(w2, u, c).wait_send()
        open_landings()

    @pl.when(feed)
    def _():
        open_landings()

    @pl.when(attention)
    def _():
        reduce_blocks(4, 0, attention_grad, attention_block, attention_landing, attention_deliver)
        for i in range(2):
            lent_weight(i).wait_send()
            feed_deliver(2 * i).copy.wait_recv()

    @pl.when(feed)
    def _():
        reduce_blocks(8, EARLY, feed_grad, feed_block, feed_landing, feed_deliver)

    for u in range(UNITS):
        @pl.when(jnp.logical_not(first))
        def _():
            for i in range(BACK_PARTS):
                backward_send(u, i).wait_send()
    norm_copy.wait()


def rotary_pieces():
    lane = np.arange(128)
    angles = np.arange(UNIT)[:, None] * 10000.0 ** (-2.0 * (lane % 32) / HEAD_DIM)
    sign = np.where(lane % HEAD_DIM < HEAD_DIM // 2, -1.0, 1.0)
    left = np.concatenate([np.cos(angles), np.sin(angles) * sign], axis=1)
    pieces = []
    for _ in range(3):
        pieces.append(left.astype(ml_dtypes.bfloat16))
        left = left - pieces[-1].astype(np.float64)
    return jnp.asarray(np.concatenate(pieces, axis=1))


def on_device(inputs, blocks, norm_gain, norm_bias, segments, cotangent):
    sections, line_size = lax.axis_size("section"), lax.axis_size("dp")
    bits = line_size.bit_length() - 1
    reduced = max(n for n in range(bits + 1) if (inputs.shape[2] >> n) % 16 == 0)
    batches, length, width = inputs.shape
    units = (UNITS, UNIT, width)
    low = lambda *shape: pltpu.VMEM(shape, BF16)
    full = lambda *shape: pltpu.VMEM(shape, F32)
    dma = lambda n: pltpu.SemaphoreType.DMA((n,))
    hbm = pl.BlockSpec(memory_space=pl.ANY)
    y, dx, grads, norms = pl.pallas_call(
        functools.partial(relay_kernel, sections, line_size, reduced),
        out_shape=(
            jax.ShapeDtypeStruct(inputs.shape, BF16),
            jax.ShapeDtypeStruct(inputs.shape, BF16),
            jax.ShapeDtypeStruct((6, width >> reduced, width), F32),
            jax.ShapeDtypeStruct((8, width), F32),
        ),
        in_specs=[hbm] * 7,
        out_specs=(hbm,) * 4,
        scratch_shapes=[
            *[low(*units) for _ in range(3)], low(4 * UNITS * UNIT, width),
            low(48, UNIT, CHUNK), low(width, 4 * width), low(4 * width, width),
            full(UNITS, UNIT, 128), full(UNITS, UNIT, 128), pltpu.VMEM((batches, 1, length), jnp.int32), low(UNIT, width),
            low(2, UNIT, 128), full(UNITS, UNIT, 128), low(UNIT, width), full(UNIT, width), low(length, width),
            full(1, width), full(1, width), full(bits + 1, 8, width), full(bits, 8, width),
            *[pltpu.SemaphoreType.DMA((UNITS, n)) for n in (PARTS, PARTS, BACK_PARTS, BACK_PARTS)], dma(2), dma(2), dma(5), dma(6), pltpu.SemaphoreType.DMA, dma(8),
            pltpu.SemaphoreType.DMA((8, reduced)), pltpu.SemaphoreType.DMA((8, reduced)), dma(2), dma(2), dma(bits), dma(bits),
            pltpu.SemaphoreType.REGULAR((bits,)),
        ],
        compiler_params=pltpu.CompilerParams(
            collective_id=1, has_side_effects=True, vmem_limit_bytes=64 * 2**20 - 8192),
        name="relay",
    )(inputs, cotangent, blocks[0], norm_gain, norm_bias, segments[:, None, :], rotary_pieces())
    if bits > reduced:
        near = 1 << (bits - reduced)
        groups = [list(range(i, i + near)) for i in range(0, line_size, near)]
        grads = lax.psum_scatter(grads, "dp", scatter_dimension=1, axis_index_groups=groups, tiled=True)
    own = width // line_size
    norms = lax.dynamic_slice_in_dim(norms, lax.axis_index("dp") * own, own, 1)
    return y[None], dx[None], grads[None], norms[0:1], norms[1:2]


def solution(mesh):
    return jax.shard_map(
        on_device,
        mesh=mesh,
        in_specs=(
            P("dp", None, None),
            P("section", None, None, None),
            P("section", None),
            P("section", None),
            P("dp", None),
            P("dp", None, None),
        ),
        out_specs=(
            P("section", "dp", None, None),
            P("section", "dp", None, None),
            P("section", None, "dp", None),
            P("section", "dp"),
            P("section", "dp"),
        ),
        check_vma=False,
    )
```
